32 devices in a mesh: segment: 4 (over y, x), dp: 8 (over z, core).
Axes of the slice: x: 2, y: 2, z: 4, core: 2. Of those that a mesh axis runs over, the one named last changes fastest.
Arguments:
- x_saved: bfloat16 [4, 1024, 1536], P('segment', 'dp'), may hold values from -6 to 6
- gains: float32 [4, 1536], P('segment'), may hold values from 0.1 to 1.9
- w_in: bfloat16 [4, 1536, 3072], P('segment', 'dp'), may hold values from -0.15625 to 0.15625
- w_out: bfloat16 [4, 3072, 1536], P('segment', None, 'dp'), may hold values from -0.109375 to 0.109375
- cotangent: bfloat16 [1024, 1536], P('dp'), may hold values from -6 to 6
- lengths: int32 [8], replicated, may hold values from 1 to 256, 1024 in all
Outputs:
- grads: bfloat16 [4, 1024, 1536], P('segment', 'dp')
- gain_grads: float32 [4, 1536], P('segment')
The draws below stay inside these ranges and needn't reach their ends.
All inputs are finite; a program needn't handle non-finite values.
Results may differ from the reference program's by a relative error of at most 0.0075.
Values may be sent and summed in bfloat16 or wider, within the bound.
A program may use at most 128 MiB of HBM per device.

```python
import math
import jax
import jax.numpy as jnp
import numpy as np
from jax import lax

D = 1536
FF = 3072
TOK_DEV = 128
TOKENS = 1024
UTTS = 8
MAXLEN = 256
N_SEGMENT = 4


def steps_of(stream_key, dims, pieces, low, largest):
    factor_of, own = 1.0, jax.random.fold_in(stream_key, 6)
    for dim, blocks in pieces:
        draws = jnp.exp(jax.random.uniform(jax.random.fold_in(own, dim), (blocks,), jnp.float32, low / len(pieces), largest / len(pieces)))
        factor_of = factor_of * jnp.repeat(draws, dims[dim] // blocks).reshape([-1 if axis == dim else 1 for axis in range(len(dims))])
    return factor_of


def length_profile(amount, total, bound, skew):
    portions = [(1 << 20) // math.isqrt(grade ** skew) + 1 for grade in range(2, amount + 1)]
    surplus, given = total - bound - (amount - 1), [1] * (amount - 1)
    while surplus > 0:
        free = [i for i in range(amount - 1) if given[i] < bound]
        whole, left = sum([portions[i] for i in free]), surplus
        for i in free:
            extra = min(bound - given[i], max(1, left * portions[i] // whole), surplus)
            given[i] = given[i] + extra
            surplus = surplus - extra
    return np.array([bound] + given)


def ragged(stream_key, count, total, limit, slope):
    if count == 2:
        one = jax.random.randint(stream_key, (), max(1, total - limit), min(limit, total - 1) + 1)
        return jnp.stack([one, total - one])
    tallies = jnp.asarray(length_profile(count, total, limit, slope), jnp.int32)
    twos = (count - 1) // 2
    source_of, taker = tallies[1:1 + 2 * twos:2], tallies[2:2 + 2 * twos:2]
    slack = jnp.minimum(source_of - 1, limit - taker)
    shifted = jax.random.randint(jax.random.fold_in(stream_key, 1), (twos,), 0, 1 << 20) % (slack + 1)
    tallies = tallies.at[1:1 + 2 * twos:2].set(source_of - shifted).at[2:2 + 2 * twos:2].set(taker + shifted)
    return tallies[jax.random.permutation(jax.random.fold_in(stream_key, 2), count)]


def noise(key, dims, deviation, reach, pieces=(), kind=jnp.bfloat16):
    gain = steps_of(key, dims, pieces, -0.22, 0.18) if pieces else 1.0
    values = jax.random.normal(key, dims, jnp.float32) * deviation * gain
    return jnp.minimum(jnp.maximum(values, -reach), reach).astype(kind)


def setup_inputs(seed: int = 0) -> dict:
    key_of = jax.random.split(jax.random.key(seed), 7)
    return {
        "x_saved": noise(key_of[0], (N_SEGMENT, TOKENS, D), 1.0, 6.0, ((0, 4), (1, 8))),
        "gains": jnp.clip(1.0 + 0.18 * jax.random.normal(key_of[1], (N_SEGMENT, D), jnp.float32), 0.1, 1.9),
        "w_in": noise(key_of[2], (N_SEGMENT, D, FF), D ** -0.5, 0.15625, ((0, 4), (1, 8))),
        "w_out": noise(key_of[3], (N_SEGMENT, FF, D), FF ** -0.5, 0.109375, ((0, 4), (2, 8))),
        "cotangent": noise(key_of[4], (TOKENS, D), 1.0, 6.0, ((0, 8),)),
        "lengths": ragged(key_of[5], UTTS, TOKENS, MAXLEN, 2).astype(jnp.int32),
    }


def segment_back(x, gain_vector, w_first, w_second, grad_in):
    xf = x.astype(jnp.float32)
    centered_input = xf - lax.optimization_barrier(jnp.mean(xf, -1, keepdims=True))
    variance = lax.optimization_barrier(jnp.mean(centered_input * centered_input, -1, keepdims=True))
    inverse_deviation = lax.rsqrt(variance + 1e-05)
    standardized_input = centered_input * inverse_deviation
    normalized_input = (standardized_input * gain_vector).astype(jnp.bfloat16)
    hidden = jnp.dot(normalized_input, w_first, preferred_element_type=jnp.float32)
    up_grad = jnp.dot(grad_in, w_second.T, preferred_element_type=jnp.float32)
    sig = jax.nn.sigmoid(hidden)
    hid_grad = (0.5 * up_grad * (sig + hidden * sig * (1.0 - sig))).astype(jnp.bfloat16)
    norm_gradient = jnp.dot(hid_grad, w_first.T, preferred_element_type=jnp.float32)
    gain_partial = lax.optimization_barrier(jnp.sum(norm_gradient * standardized_input, 0))
    gain_scaled = norm_gradient * gain_vector
    backward_result = inverse_deviation * (gain_scaled - lax.optimization_barrier(jnp.mean(gain_scaled, -1, keepdims=True)) - standardized_input * lax.optimization_barrier(jnp.mean(gain_scaled * standardized_input, -1, keepdims=True)))
    return ((grad_in.astype(jnp.float32) + backward_result).astype(jnp.bfloat16), gain_partial)

def reference(x_saved, gains, w_in, w_out, cotangent, lengths):
    ends = jnp.cumsum(lengths)
    position = jnp.arange(TOKENS, dtype=jnp.int32)
    utter = lax.optimization_barrier(jnp.sum((position[:, None] >= ends[None, :]).astype(jnp.int32), 1))
    tok_len = jnp.take(lengths, utter).astype(jnp.float32)
    weight = 2.0 * TOK_DEV / (tok_len + TOK_DEV)
    current = (cotangent.astype(jnp.float32) * weight[:, None]).astype(jnp.bfloat16)
    grad_list = []
    gain_list = []
    for level in range(N_SEGMENT - 1, -1, -1):
        current, gain_partial = segment_back(x_saved[level], gains[level], w_in[level], w_out[level], current)
        grad_list.insert(0, current)
        gain_list.insert(0, gain_partial)
    return (jnp.stack(grad_list), jnp.stack(gain_list))
```

```python
import functools

import jax
import jax.numpy as jnp
from jax import lax
from jax.experimental import pallas as pl
from jax.experimental.pallas import tpu as pltpu
from jax.sharding import PartitionSpec as P

MESH = pl.DeviceIdType.MESH
PIECES = 6
CHUNK = 128


def passed_along(x, axis, by):
    length = lax.axis_size(axis)
    pairs = [(i, i + by) for i in range(length) if 0 <= i + by < length]
    return lax.ppermute(x, axis, pairs)


def on_device(x_saved, gains, w_in, w_out, cotangent, lengths):
    rows = cotangent.shape[0]
    width = cotangent.shape[1]
    ends = jnp.cumsum(lengths)
    position = lax.axis_index("dp") * rows + jnp.arange(rows, dtype=jnp.int32)
    utter_hit = (position[:, None] >= ends[None, :]).astype(jnp.int32)
    utter = jnp.sum(utter_hit, 1)
    onehot = (utter[:, None] == jnp.arange(lengths.shape[0], dtype=jnp.int32)[None, :]).astype(
        jnp.int32
    )
    tok_len = jnp.sum(onehot * lengths[None, :], 1).astype(jnp.float32)
    weight = 2.0 * rows / (tok_len + rows)
    current = (cotangent.astype(jnp.float32) * weight[:, None]).astype(jnp.bfloat16)
    xf = x_saved[0].astype(jnp.float32)
    centered_input = xf - jnp.mean(xf, -1, keepdims=True)
    variance = jnp.mean(centered_input * centered_input, -1, keepdims=True)
    inverse_deviation = lax.rsqrt(variance + 1e-05)
    standardized_input = centered_input * inverse_deviation
    gain_vector = gains[0]
    normalized_input = (standardized_input * gain_vector).astype(jnp.bfloat16)
    w_first, w_second = (
        lax.all_gather(w_in[0], "dp", axis=0, tiled=True),
        lax.all_gather(w_out[0].T, "dp", axis=0, tiled=True).T,
    )

    def project_all(normed_rows, grad_in):
        hidden = jnp.dot(normed_rows, w_first, preferred_element_type=jnp.float32)
        up_grad = jnp.dot(grad_in, w_second.T, preferred_element_type=jnp.float32)
        sig = jax.nn.sigmoid(hidden)
        hid_grad = (0.5 * up_grad * (sig + hidden * sig * (1.0 - sig))).astype(jnp.bfloat16)
        return jnp.dot(hid_grad, w_first.T, preferred_element_type=jnp.float32)

    def block_back(grad_in):
        norm_gradient = project_all(normalized_input, grad_in)
        gain_partial = jnp.sum(norm_gradient * standardized_input, 0)
        gain_scaled = norm_gradient * gain_vector
        backward_result = inverse_deviation * (
            gain_scaled
            - jnp.mean(gain_scaled, -1, keepdims=True)
            - standardized_input * jnp.mean(gain_scaled * standardized_input, -1, keepdims=True)
        )
        return (
            (grad_in.astype(jnp.float32) + backward_result).astype(jnp.bfloat16),
            gain_partial,
        )

    def pass_through(grad_in):
        return (grad_in, jnp.zeros((width,), jnp.float32))

    segments = lax.axis_size("segment")
    my_segment = lax.axis_index("segment")
    gain_local = jnp.zeros((width,), jnp.float32)
    result = current
    for level in range(segments - 1, -1, -1):
        mine = my_segment == level
        updated, gain_partial = lax.cond(mine, block_back, pass_through, current)
        result = jnp.where(mine, updated, result)
        gain_local = jnp.where(mine, gain_partial, gain_local)
        if level > 0:
            current = passed_along(updated, "segment", -1)
    gain_total = lax.psum(gain_local, "dp")
    return (result[None], gain_total[None])


def kernel(
    segments, utts,
    x_ref, gain_ref, wst_ref, cot_ref, len_ref, out_ref, gg_ref,
    W, F, dz, xh, zb, g, gn, inv, xin, slots,
    lsem, hs, hr, os_, or_, fs, fr, ps, pr, xs, xr, ts, tr, gs, gr, rs, rr, qs, qr,
):
    D = x_ref.shape[1]
    T = x_ref.shape[0]
    depth = wst_ref.shape[1]
    FF = wst_ref.shape[2]
    blk = FF // PIECES
    R2 = 2 * T
    n_chunks = R2 // CHUNK

    s = lax.axis_index("segment")
    k = lax.axis_index("dp")
    z = k // 2
    c = k % 2
    worker = (z == 1) | (z == 2)
    helper = (z == 0) | (z == 3)
    top_seg = s == segments - 1
    zw = 1 + z // 2
    zh = 3 * (z // 2)
    zo = 3 - zw
    zoh = 3 - zh
    partner = 2 * z + (1 - c)
    sources = (zw, zh, zo, zoh)

    barrier = pltpu.get_barrier_semaphore()
    for d in range(1, 8):
        pl.semaphore_signal(
            barrier, inc=1, device_id={"dp": lax.rem(k + d, 8)}, device_id_type=MESH
        )

    @pl.when(s > 0)
    def _():
        pl.semaphore_signal(barrier, inc=1, device_id={"segment": s - 1}, device_id_type=MESH)

    @pl.when(s < segments - 1)
    def _():
        pl.semaphore_signal(barrier, inc=1, device_id={"segment": s + 1}, device_id_type=MESH)

    near = (s > 0).astype(jnp.int32) + (s < segments - 1).astype(jnp.int32)
    pl.semaphore_wait(barrier, 7 + near)

    def rows_of(zz, cc):
        return pl.ds(pl.multiple_of((2 * zz + cc) * depth, depth), depth)

    def cols_of(p):
        return pl.ds(pl.multiple_of(p * blk, blk), blk)

    def remote(src, dst, ssem, rsem, dev):
        return pltpu.make_async_remote_copy(
            src_ref=src, dst_ref=dst, send_sem=ssem, recv_sem=rsem,
            device_id=dev, device_id_type=MESH,
        )

    def own_src(p):
        return wst_ref.at[:, :, cols_of(p)]

    def slot(zz, cc, p):
        return W.at[:, rows_of(zz, cc), cols_of(p)]

    def to_worker(p):
        return remote(own_src(p), slot(z, c, p), hs.at[p], hr.at[p], {"dp": 2 * zw + c})

    def from_helper(p):
        return remote(slot(zh, c, p), slot(zh, c, p), hs.at[p], hr.at[p], {"dp": 2 * zh + c})

    def own_to_other(p):
        return remote(own_src(p), slot(z, c, p), os_.at[p], or_.at[p], {"dp": 2 * zo + c})

    def own_from_other(p):
        return remote(own_src(p), slot(zo, c, p), os_.at[p], or_.at[p], {"dp": 2 * zo + c})

    def fwd_to_other(p):
        return remote(slot(zh, c, p), slot(zh, c, p), fs.at[p], fr.at[p], {"dp": 2 * zo + c})

    def fwd_from_other(p):
        return remote(slot(zoh, c, p), slot(zoh, c, p), fs.at[p], fr.at[p], {"dp": 2 * zo + c})

    def to_partner(i, p):
        src = own_src(p) if i == 0 else slot(sources[i], c, p)
        return remote(src, slot(sources[i], c, p), ps.at[i, p], pr.at[i, p], {"dp": partner})

    def from_partner(i, p):
        there = slot(sources[i], 1 - c, p)
        return remote(there, there, ps.at[i, p], pr.at[i, p], {"dp": partner})

    local = pltpu.make_async_copy(wst_ref, W.at[:, rows_of(z, c), :], lsem)
    top_rows = g.at[pl.ds(T, T), :]
    x_send = remote(x_ref, xin.at[pl.ds(0, T), :], xs, xr, {"dp": 2 * zw + c})
    x_recv = remote(x_ref, xin.at[pl.ds(0, T), :], xs, xr, {"dp": 2 * zh + c})
    t_send = remote(top_rows, g.at[pl.ds(0, T), :], ts, tr, {"dp": 2 * zw + c})
    t_recv = remote(top_rows, g.at[pl.ds(0, T), :], ts, tr, {"dp": 2 * zh + c})
    ret_send = remote(gn.at[pl.ds(0, T), :], gn.at[pl.ds(T, T), :], rs, rr, {"dp": 2 * zh + c})
    ret_recv = remote(gn.at[pl.ds(0, T), :], gn.at[pl.ds(T, T), :], rs, rr, {"dp": 2 * zw + c})

    @pl.when(helper)
    def _():
        x_send.start()

    @pl.when(worker)
    def _():
        own_to_other(0).start()
        to_partner(0, 0).start()
        local.start()

    @pl.when(top_seg)
    def _():
        pos = k * T + lax.broadcasted_iota(jnp.int32, (T, 128), 0)
        tok = jnp.zeros((T, 128), jnp.float32)
        start = jnp.int32(0)
        for j in range(utts):
            n = len_ref[j]
            hit = (pos >= start) & (pos < start + n)
            tok = jnp.where(hit, n.astype(jnp.float32), tok)
            start = start + n
        weight = (2.0 * T / (tok + T))[:, 0:1]
        g[T:, :] = (cot_ref[...].astype(jnp.float32) * weight).astype(jnp.bfloat16)

    @pl.when(helper & top_seg)
    def _():
        t_send.start()

    @pl.when(helper)
    def _():
        @pl.loop(0, PIECES)
        def _(p):
            to_worker(p).start()

    NORM = 64

    @pl.when(worker)
    def _():
        xin[T:, :] = x_ref[...]
        x_recv.wait_recv()

        @pl.loop(0, R2 // NORM)
        def _(i):
            r = pl.ds(pl.multiple_of(i * NORM, NORM), NORM)
            xf = xin[r, :].astype(jnp.float32)
            cen = xf - jnp.mean(xf, -1, keepdims=True)
            iv = lax.rsqrt(jnp.mean(cen * cen, -1, keepdims=True) + 1e-05)
            xhat = cen * iv
            inv[r, :] = jnp.broadcast_to(iv, (NORM, 128))
            xh[r, :] = xhat
            zb[r, :] = (xhat * gain_ref[...]).astype(jnp.bfloat16)
            dz[r, :] = jnp.zeros((NORM, D), jnp.float32)

        @pl.when(top_seg)
        def _():
            t_recv.wait_recv()

        local.wait()

    def hidden(p):
        h = jnp.dot(zb[...], W[0, :, cols_of(p)], preferred_element_type=jnp.float32)
        sig = jax.nn.sigmoid(h)
        F[:, cols_of(p)] = 0.5 * (sig + h * sig * (1.0 - sig))

    def back(p, r):
        u = jnp.dot(g[r, :], W[1, :, cols_of(p)], preferred_element_type=jnp.float32)
        du = (u * F[r, cols_of(p)]).astype(jnp.bfloat16)
        dz[r, :] += lax.dot_general(
            du, W[0, :, cols_of(p)], (((1,), (1,)), ((), ())),
            preferred_element_type=jnp.float32,
        )

    @pl.when(worker)
    def _():
        @pl.loop(0, PIECES)
        def _(p):
            @pl.when(p + 1 < PIECES)
            def _():
                own_to_other(p + 1).start()
                to_partner(0, p + 1).start()

            from_helper(p).wait_recv()
            fwd_to_other(p).start()
            to_partner(1, p).start()
            own_from_other(p).wait_recv()
            to_partner(2, p).start()
            fwd_from_other(p).wait_recv()
            to_partner(3, p).start()
            for i in range(4):
                from_partner(i, p).wait_recv()
            hidden(p)

            @pl.when(top_seg)
            def _():
                back(p, pl.ds(0, R2))

    def g_copy(i, to):
        r = pl.ds(pl.multiple_of(i * CHUNK, CHUNK), CHUNK)
        return remote(gn.at[r, :], g.at[r, :], gs.at[i], gr.at[i], {"segment": to})

    wi = jnp.clip((z - 1) * 2 + c, 0, 3)
    EP = 64

    @pl.when(worker)
    def _():
        slots[wi] = jnp.zeros((1, D), jnp.float32)

        @pl.loop(0, n_chunks)
        def _(i):
            r = pl.ds(pl.multiple_of(i * CHUNK, CHUNK), CHUNK)

            @pl.when(jnp.logical_not(top_seg))
            def _():
                g_copy(i, s + 1).wait_recv()

                @pl.loop(0, PIECES)
                def _(p):
                    back(p, r)

            @pl.loop(0, CHUNK // EP)
            def _(j):
                q = pl.ds(pl.multiple_of(i * CHUNK + j * EP, EP), EP)
                d = dz[q, :]
                xhat = xh[q, :]
                t = d * xhat
                slots[wi] += jnp.sum(t, 0, keepdims=True)
                gain = gain_ref[...]
                e = d * gain
                m1 = jnp.mean(e, -1, keepdims=True)
                m2 = jnp.mean(t * gain, -1, keepdims=True)
                gn[q, :] = (
                    g[q, :].astype(jnp.float32) + inv[q, 0:1] * (e - m1 - xhat * m2)
                ).astype(jnp.bfloat16)

            @pl.when(s > 0)
            def _():
                g_copy(i, s - 1).start()

            @pl.when((i + 1) * CHUNK == T)
            def _():
                ret_send.start()

    def q_copy(d):
        return remote(slots.at[wi], slots.at[wi], qs.at[d], qr.at[wi], {"dp": lax.rem(k + d, 8)})

    @pl.when(worker)
    def _():
        for d in range(1, 8):
            q_copy(d).start()
        out_ref[...] = gn[T:, :]

    @pl.when(helper)
    def _():
        ret_recv.wait_recv()
        out_ref[...] = gn[T:, :]

    for w in range(4):
        @pl.when(k != w + 2)
        def _(w=w):
            remote(
                slots.at[w], slots.at[w], qs.at[0], qr.at[w], {"dp": partner}
            ).wait_recv()

    gg_ref[...] = slots[0] + slots[1] + slots[2] + slots[3]

    @pl.when(worker)
    def _():
        for d in range(1, 8):
            q_copy(d).wait_send()
        ret_send.wait_send()

        @pl.loop(0, PIECES)
        def _(p):
            own_to_other(p).wait_send()
            fwd_to_other(p).wait_send()
            for i in range(4):
                to_partner(i, p).wait_send()

        @pl.when(s > 0)
        def _():
            @pl.loop(0, n_chunks)
            def _(i):
                g_copy(i, s - 1).wait_send()

    @pl.when(helper)
    def _():
        x_send.wait_send()

        @pl.loop(0, PIECES)
        def _(p):
            to_worker(p).wait_send()

        @pl.when(top_seg)
        def _():
            t_send.wait_send()


def in_kernel(segments, x_saved, gains, w_in, w_out, cotangent, lengths):
    T, D = cotangent.shape
    FF = w_in.shape[2]
    wst = jnp.stack([w_in[0], w_out[0].T])
    R2 = 2 * T
    DMA = pltpu.SemaphoreType.DMA
    bf, f32 = jnp.bfloat16, jnp.float32
    vmem = pl.BlockSpec(memory_space=pltpu.VMEM)
    grads, gg = pl.pallas_call(
        functools.partial(kernel, segments, lengths.shape[0]),
        out_shape=(jax.ShapeDtypeStruct((T, D), bf), jax.ShapeDtypeStruct((1, D), f32)),
        in_specs=[
            vmem, vmem, pl.BlockSpec(memory_space=pl.ANY), vmem,
            pl.BlockSpec(memory_space=pltpu.SMEM),
        ],
        out_specs=(vmem, vmem),
        scratch_shapes=[
            pltpu.VMEM((2, D, FF), bf),
            pltpu.VMEM((R2, FF), f32),
            pltpu.VMEM((R2, D), f32),
            pltpu.VMEM((R2, D), f32),
            pltpu.VMEM((R2, D), bf),
            pltpu.VMEM((R2, D), bf),
            pltpu.VMEM((R2, D), bf),
            pltpu.VMEM((R2, 128), f32),
            pltpu.VMEM((R2, D), bf),
            pltpu.VMEM((4, 1, D), f32),
            DMA, DMA((PIECES,)), DMA((PIECES,)), DMA((PIECES,)), DMA((PIECES,)),
            DMA((PIECES,)), DMA((PIECES,)), DMA((4, PIECES)), DMA((4, PIECES)),
            DMA, DMA, DMA, DMA, DMA((R2 // CHUNK,)), DMA((R2 // CHUNK,)),
            DMA, DMA, DMA((8,)), DMA((4,)),
        ],
        compiler_params=pltpu.CompilerParams(
            collective_id=0, has_side_effects=True, vmem_limit_bytes=56 * 1024 * 1024
        ),
    )(x_saved[0], gains, wst, cotangent, lengths)
    return (grads[None], gg)


def solution(mesh):
    in_specs = (
        P("segment", "dp", None),
        P("segment", None),
        P("segment", "dp", None),
        P("segment", None, "dp"),
        P("dp", None),
        P(),
    )
    out_specs = (P("segment", "dp", None), P("segment", None))
    body = on_device
    if mesh.shape["dp"] == 8:
        body = functools.partial(in_kernel, mesh.shape["segment"])
    return jax.shard_map(
        body, mesh=mesh, in_specs=in_specs, out_specs=out_specs, check_vma=False
    )
```

```python
import functools

import jax
import jax.numpy as jnp
from jax import lax
from jax.experimental import pallas as pl
from jax.experimental.pallas import tpu as pltpu
from jax.sharding import PartitionSpec as P

MESH = pl.DeviceIdType.MESH
PIECES = 4
CHUNK = 64


def passed_along(x, axis, by):
    length = lax.axis_size(axis)
    pairs = [(i, i + by) for i in range(length) if 0 <= i + by < length]
    return lax.ppermute(x, axis, pairs)


def on_device(x_saved, gains, w_in, w_out, cotangent, lengths):
    rows = cotangent.shape[0]
    width = cotangent.shape[1]
    index = jnp.arange(lengths.shape[0], dtype=jnp.int32)
    ends = jnp.sum(jnp.where(index[:, None] <= index[None, :], lengths[:, None], 0), 0)
    position = lax.axis_index("dp") * rows + jnp.arange(rows, dtype=jnp.int32)
    utter_hit = (position[:, None] >= ends[None, :]).astype(jnp.int32)
    utter = jnp.sum(utter_hit, 1)
    onehot = (utter[:, None] == jnp.arange(lengths.shape[0], dtype=jnp.int32)[None, :]).astype(
        jnp.int32
    )
    tok_len = jnp.sum(onehot * lengths[None, :], 1).astype(jnp.float32)
    weight = 2.0 * rows / (tok_len + rows)
    current = (cotangent.astype(jnp.float32) * weight[:, None]).astype(jnp.bfloat16)
    xf = x_saved[0].astype(jnp.float32)
    centered_input = xf - jnp.mean(xf, -1, keepdims=True)
    variance = jnp.mean(centered_input * centered_input, -1, keepdims=True)
    inverse_deviation = lax.rsqrt(variance + 1e-05)
    standardized_input = centered_input * inverse_deviation
    gain_vector = gains[0]
    normalized_input = (standardized_input * gain_vector).astype(jnp.bfloat16)
    w_first, w_second = (
        lax.all_gather(w_in[0], "dp", axis=0, tiled=True),
        lax.all_gather(w_out[0].T, "dp", axis=0, tiled=True).T,
    )

    def project_all(normed_rows, grad_in):
        hidden = jnp.dot(normed_rows, w_first, preferred_element_type=jnp.float32)
        up_grad = jnp.dot(grad_in, w_second.T, preferred_element_type=jnp.float32)
        sig = jax.nn.sigmoid(hidden)
        hid_grad = (0.5 * up_grad * (sig + hidden * sig * (1.0 - sig))).astype(jnp.bfloat16)
        return jnp.dot(hid_grad, w_first.T, preferred_element_type=jnp.float32)

    def block_back(grad_in):
        norm_gradient = project_all(normalized_input, grad_in)
        gain_partial = jnp.sum(norm_gradient * standardized_input, 0)
        gain_scaled = norm_gradient * gain_vector
        backward_result = inverse_deviation * (
            gain_scaled
            - jnp.mean(gain_scaled, -1, keepdims=True)
            - standardized_input * jnp.mean(gain_scaled * standardized_input, -1, keepdims=True)
        )
        return (
            (grad_in.astype(jnp.float32) + backward_result).astype(jnp.bfloat16),
            gain_partial,
        )

    def pass_through(grad_in):
        return (grad_in, jnp.zeros((width,), jnp.float32))

    segments = lax.axis_size("segment")
    my_segment = lax.axis_index("segment")
    gain_local = jnp.zeros((width,), jnp.float32)
    result = current
    for level in range(segments - 1, -1, -1):
        mine = my_segment == level
        updated, gain_partial = lax.cond(mine, block_back, pass_through, current)
        result = jnp.where(mine, updated, result)
        gain_local = jnp.where(mine, gain_partial, gain_local)
        if level > 0:
            current = passed_along(updated, "segment", -1)
    gain_total = lax.psum(gain_local, "dp")
    return (result[None], gain_total[None])


def kernel(
    segments, utts,
    x_ref, gain_ref, wst_ref, cot_ref, len_ref, out_ref, gg_ref,
    W, F, dz, xh, zb, g, gn, inv, xin, slots,
    lsem, hs, hr, os_, or_, fs, fr, ps, pr, xs, xr, ts, tr, gs, gr, rs, rr, qs, qr,
):
    D = x_ref.shape[1]
    T = x_ref.shape[0]
    depth = wst_ref.shape[2]
    FF = F.shape[1]
    blk = FF // PIECES
    R2 = 2 * T
    n_chunks = R2 // CHUNK

    s = lax.axis_index("segment")
    k = lax.axis_index("dp")
    z = k // 2
    c = k % 2
    worker = (z == 1) | (z == 2)
    helper = (z == 0) | (z == 3)
    top_seg = s == segments - 1
    zw = 1 + z // 2
    zh = 3 * (z // 2)
    zo = 3 - zw
    zoh = 3 - zh
    partner = 2 * z + (1 - c)
    sources = (zw, zh, zo, zoh)

    barrier = pltpu.get_barrier_semaphore()
    for d in range(1, 8):
        pl.semaphore_signal(
            barrier, inc=1, device_id={"dp": lax.rem(k + d, 8)}, device_id_type=MESH
        )

    @pl.when(s > 0)
    def _():
        pl.semaphore_signal(barrier, inc=1, device_id={"segment": s - 1}, device_id_type=MESH)

    @pl.when(s < segments - 1)
    def _():
        pl.semaphore_signal(barrier, inc=1, device_id={"segment": s + 1}, device_id_type=MESH)

    near = (s > 0).astype(jnp.int32) + (s < segments - 1).astype(jnp.int32)
    pl.semaphore_wait(barrier, 7 + near)

    def rows_of(zz, cc):
        return pl.ds(pl.multiple_of((2 * zz + cc) * depth, depth), depth)

    def cols_of(p):
        return pl.ds(pl.multiple_of(p * blk, blk), blk)

    def remote(src, dst, ssem, rsem, dev):
        return pltpu.make_async_remote_copy(
            src_ref=src, dst_ref=dst, send_sem=ssem, recv_sem=rsem,
            device_id=dev, device_id_type=MESH,
        )

    def own_src(p):
        return wst_ref.at[p]

    def slot(zz, cc, p):
        return W.at[p, :, rows_of(zz, cc), :]

    def to_worker(p):
        return remote(own_src(p), slot(z, c, p), hs.at[p], hr.at[p], {"dp": 2 * zw + c})

    def from_helper(p):
        return remote(slot(zh, c, p), slot(zh, c, p), hs.at[p], hr.at[p], {"dp": 2 * zh + c})

    def own_to_other(p):
        return remote(own_src(p), slot(z, c, p), os_.at[p], or_.at[p], {"dp": 2 * zo + c})

    def own_from_other(p):
        return remote(own_src(p), slot(zo, c, p), os_.at[p], or_.at[p], {"dp": 2 * zo + c})

    def fwd_to_other(p):
        return remote(slot(zh, c, p), slot(zh, c, p), fs.at[p], fr.at[p], {"dp": 2 * zo + c})

    def fwd_from_other(p):
        return remote(slot(zoh, c, p), slot(zoh, c, p), fs.at[p], fr.at[p], {"dp": 2 * zo + c})

    def to_partner(i, p):
        src = own_src(p) if i == 0 else slot(sources[i], c, p)
        return remote(src, slot(sources[i], c, p), ps.at[i, p], pr.at[i, p], {"dp": partner})

    def from_partner(i, p):
        there = slot(sources[i], 1 - c, p)
        return remote(there, there, ps.at[i, p], pr.at[i, p], {"dp": partner})

    local = pltpu.make_async_copy(wst_ref, W.at[:, :, rows_of(z, c), :], lsem)
    top_rows = g.at[pl.ds(T, T), :]
    x_send = remote(x_ref, xin.at[pl.ds(0, T), :], xs, xr, {"dp": 2 * zw + c})
    x_recv = remote(x_ref, xin.at[pl.ds(0, T), :], xs, xr, {"dp": 2 * zh + c})
    t_send = remote(top_rows, g.at[pl.ds(0, T), :], ts, tr, {"dp": 2 * zw + c})
    t_recv = remote(top_rows, g.at[pl.ds(0, T), :], ts, tr, {"dp": 2 * zh + c})
    ret_send = remote(gn.at[pl.ds(0, T), :], gn.at[pl.ds(T, T), :], rs, rr, {"dp": 2 * zh + c})
    ret_recv = remote(gn.at[pl.ds(0, T), :], gn.at[pl.ds(T, T), :], rs, rr, {"dp": 2 * zw + c})

    @pl.when(helper)
    def _():
        x_send.start()

    @pl.when(worker)
    def _():
        own_to_other(0).start()
        to_partner(0, 0).start()
        own_to_other(1).start()
        to_partner(0, 1).start()
        local.start()

    @pl.when(top_seg)
    def _():
        pos = k * T + lax.broadcasted_iota(jnp.int32, (T, 128), 0)
        tok = jnp.zeros((T, 128), jnp.float32)
        start = jnp.int32(0)
        for j in range(utts):
            n = len_ref[j]
            hit = (pos >= start) & (pos < start + n)
            tok = jnp.where(hit, n.astype(jnp.float32), tok)
            start = start + n
        weight = (2.0 * T / (tok + T))[:, 0:1]
        g[T:, :] = (cot_ref[...].astype(jnp.float32) * weight).astype(jnp.bfloat16)

    @pl.when(helper & top_seg)
    def _():
        t_send.start()

    @pl.when(helper)
    def _():
        @pl.loop(0, PIECES)
        def _(p):
            to_worker(p).start()

    NORM = 64

    @pl.when(worker)
    def _():
        xin[T:, :] = x_ref[...]
        x_recv.wait_recv()

        @pl.loop(0, R2 // NORM)
        def _(i):
            r = pl.ds(pl.multiple_of(i * NORM, NORM), NORM)
            xf = xin[r, :].astype(jnp.float32)
            cen = xf - jnp.mean(xf, -1, keepdims=True)
            iv = lax.rsqrt(jnp.mean(cen * cen, -1, keepdims=True) + 1e-05)
            xhat = cen * iv
            inv[r, :] = jnp.broadcast_to(iv, (NORM, 128))
            xh[r, :] = xhat
            zb[r, :] = (xhat * gain_ref[...]).astype(jnp.bfloat16)
            dz[r, :] = jnp.zeros((NORM, D), jnp.float32)

        @pl.when(top_seg)
        def _():
            t_recv.wait_recv()

        local.wait()

    def hidden(p):
        h = jnp.dot(zb[...], W[p, 0], preferred_element_type=jnp.float32)
        sig = jax.nn.sigmoid(h)
        F[:, cols_of(p)] = 0.5 * (sig + h * sig * (1.0 - sig))

    def back(p, r):
        u = jnp.dot(g[r, :], W[p, 1], preferred_element_type=jnp.float32)
        du = (u * F[r, cols_of(p)]).astype(jnp.bfloat16)
        dz[r, :] += lax.dot_general(
            du, W[p, 0], (((1,), (1,)), ((), ())),
            preferred_element_type=jnp.float32,
        )

    def piece(p):
        for i in range(4):
            from_partner(i, p).wait_recv()
        hidden(p)

        @pl.when(top_seg)
        def _():
            back(p, pl.ds(0, R2))

    @pl.when(worker)
    def _():
        @pl.loop(0, PIECES)
        def _(p):
            @pl.when(p + 2 < PIECES)
            def _():
                own_to_other(p + 2).start()
                to_partner(0, p + 2).start()

            from_helper(p).wait_recv()
            fwd_to_other(p).start()
            to_partner(1, p).start()
            own_from_other(p).wait_recv()
            to_partner(2, p).start()
            fwd_from_other(p).wait_recv()
            to_partner(3, p).start()
            @pl.when(p > 0)
            def _():
                piece(p - 1)

        piece(PIECES - 1)

    def g_copy(i, to):
        r = pl.ds(pl.multiple_of(i * CHUNK, CHUNK), CHUNK)
        return remote(gn.at[r, :], g.at[r, :], gs.at[i], gr.at[i], {"segment": to})

    wi = jnp.clip((z - 1) * 2 + c, 0, 3)
    EP = 64

    @pl.when(worker)
    def _():
        slots[wi] = jnp.zeros((1, D), jnp.float32)

        @pl.loop(0, n_chunks)
        def _(i):
            r = pl.ds(pl.multiple_of(i * CHUNK, CHUNK), CHUNK)

            @pl.when(jnp.logical_not(top_seg))
            def _():
                g_copy(i, s + 1).wait_recv()

                @pl.loop(0, PIECES)
                def _(p):
                    back(p, r)

            @pl.loop(0, CHUNK // EP)
            def _(j):
                q = pl.ds(pl.multiple_of(i * CHUNK + j * EP, EP), EP)
                d = dz[q, :]
                xhat = xh[q, :]
                t = d * xhat
                slots[wi] += jnp.sum(t, 0, keepdims=True)
                gain = gain_ref[...]
                e = d * gain
                m1 = jnp.mean(e, -1, keepdims=True)
                m2 = jnp.mean(t * gain, -1, keepdims=True)
                gn[q, :] = (
                    g[q, :].astype(jnp.float32) + inv[q, 0:1] * (e - m1 - xhat * m2)
                ).astype(jnp.bfloat16)

            @pl.when(s > 0)
            def _():
                g_copy(i, s - 1).start()

            @pl.when((i + 1) * CHUNK == T)
            def _():
                ret_send.start()

    def q_copy(d):
        return remote(slots.at[wi], slots.at[wi], qs.at[d], qr.at[wi], {"dp": lax.rem(k + d, 8)})

    @pl.when(worker)
    def _():
        for d in range(1, 8):
            q_copy(d).start()
        out_ref[...] = gn[T:, :]

    @pl.when(helper)
    def _():
        ret_recv.wait_recv()
        out_ref[...] = gn[T:, :]

    for w in range(4):
        @pl.when(k != w + 2)
        def _(w=w):
            remote(
                slots.at[w], slots.at[w], qs.at[0], qr.at[w], {"dp": partner}
            ).wait_recv()

    gg_ref[...] = slots[0] + slots[1] + slots[2] + slots[3]

    @pl.when(worker)
    def _():
        for d in range(1, 8):
            q_copy(d).wait_send()
        ret_send.wait_send()

        @pl.loop(0, PIECES)
        def _(p):
            own_to_other(p).wait_send()
            fwd_to_other(p).wait_send()
            for i in range(4):
                to_partner(i, p).wait_send()

        @pl.when(s > 0)
        def _():
            @pl.loop(0, n_chunks)
            def _(i):
                g_copy(i, s - 1).wait_send()

    @pl.when(helper)
    def _():
        x_send.wait_send()

        @pl.loop(0, PIECES)
        def _(p):
            to_worker(p).wait_send()

        @pl.when(top_seg)
        def _():
            t_send.wait_send()


def in_kernel(segments, x_saved, gains, w_in, w_out, cotangent, lengths):
    T, D = cotangent.shape
    FF = w_in.shape[2]
    wst = jnp.stack(
        [
            w_in[0].reshape(-1, PIECES, FF // PIECES).transpose(1, 0, 2),
            w_out[0].reshape(PIECES, FF // PIECES, -1).transpose(0, 2, 1),
        ],
        1,
    )
    R2 = 2 * T
    DMA = pltpu.SemaphoreType.DMA
    bf, f32 = jnp.bfloat16, jnp.float32
    vmem = pl.BlockSpec(memory_space=pltpu.VMEM)
    grads, gg = pl.pallas_call(
        functools.partial(kernel, segments, lengths.shape[0]),
        out_shape=(jax.ShapeDtypeStruct((T, D), bf), jax.ShapeDtypeStruct((1, D), f32)),
        in_specs=[
            vmem, vmem, pl.BlockSpec(memory_space=pl.ANY), vmem,
            pl.BlockSpec(memory_space=pltpu.SMEM),
        ],
        out_specs=(vmem, vmem),
        scratch_shapes=[
            pltpu.VMEM((PIECES, 2, D, FF // PIECES), bf),
            pltpu.VMEM((R2, FF), f32),
            pltpu.VMEM((R2, D), f32),
            pltpu.VMEM((R2, D), f32),
            pltpu.VMEM((R2, D), bf),
            pltpu.VMEM((R2, D), bf),
            pltpu.VMEM((R2, D), bf),
            pltpu.VMEM((R2, 128), f32),
            pltpu.VMEM((R2, D), bf),
            pltpu.VMEM((4, 1, D), f32),
            DMA, DMA((PIECES,)), DMA((PIECES,)), DMA((PIECES,)), DMA((PIECES,)),
            DMA((PIECES,)), DMA((PIECES,)), DMA((4, PIECES)), DMA((4, PIECES)),
            DMA, DMA, DMA, DMA, DMA((R2 // CHUNK,)), DMA((R2 // CHUNK,)),
            DMA, DMA, DMA((8,)), DMA((4,)),
        ],
        compiler_params=pltpu.CompilerParams(
            collective_id=0, has_side_effects=True, vmem_limit_bytes=56 * 1024 * 1024
        ),
    )(x_saved[0], gains, wst, cotangent, lengths)
    return (grads[None], gg)


def solution(mesh):
    in_specs = (
        P("segment", "dp", None),
        P("segment", None),
        P("segment", "dp", None),
        P("segment", None, "dp"),
        P("dp", None),
        P(),
    )
    out_specs = (P("segment", "dp", None), P("segment", None))
    body = on_device
    if mesh.shape["dp"] == 8:
        body = functools.partial(in_kernel, mesh.shape["segment"])
    return jax.shard_map(
        body, mesh=mesh, in_specs=in_specs, out_specs=out_specs, check_vma=False
    )
```

```python
import functools

import jax
import jax.numpy as jnp
from jax import lax
from jax.experimental import pallas as pl
from jax.experimental.pallas import tpu as pltpu
from jax.sharding import PartitionSpec as P

MESH = pl.DeviceIdType.MESH
PIECES = 2
CHUNK = 64


def passed_along(x, axis, by):
    length = lax.axis_size(axis)
    pairs = [(i, i + by) for i in range(length) if 0 <= i + by < length]
    return lax.ppermute(x, axis, pairs)


def on_device(x_saved, gains, w_in, w_out, cotangent, lengths):
    rows = cotangent.shape[0]
    width = cotangent.shape[1]
    index = jnp.arange(lengths.shape[0], dtype=jnp.int32)
    ends = jnp.sum(jnp.where(index[:, None] <= index[None, :], lengths[:, None], 0), 0)
    position = lax.axis_index("dp") * rows + jnp.arange(rows, dtype=jnp.int32)
    utter_hit = (position[:, None] >= ends[None, :]).astype(jnp.int32)
    utter = jnp.sum(utter_hit, 1)
    onehot = (utter[:, None] == jnp.arange(lengths.shape[0], dtype=jnp.int32)[None, :]).astype(
        jnp.int32
    )
    tok_len = jnp.sum(onehot * lengths[None, :], 1).astype(jnp.float32)
    weight = 2.0 * rows / (tok_len + rows)
    current = (cotangent.astype(jnp.float32) * weight[:, None]).astype(jnp.bfloat16)
    xf = x_saved[0].astype(jnp.float32)
    centered_input = xf - jnp.mean(xf, -1, keepdims=True)
    variance = jnp.mean(centered_input * centered_input, -1, keepdims=True)
    inverse_deviation = lax.rsqrt(variance + 1e-05)
    standardized_input = centered_input * inverse_deviation
    gain_vector = gains[0]
    normalized_input = (standardized_input * gain_vector).astype(jnp.bfloat16)
    w_first, w_second = (
        lax.all_gather(w_in[0], "dp", axis=0, tiled=True),
        lax.all_gather(w_out[0].T, "dp", axis=0, tiled=True).T,
    )

    def project_all(normed_rows, grad_in):
        hidden = jnp.dot(normed_rows, w_first, preferred_element_type=jnp.float32)
        up_grad = jnp.dot(grad_in, w_second.T, preferred_element_type=jnp.float32)
        sig = jax.nn.sigmoid(hidden)
        hid_grad = (0.5 * up_grad * (sig + hidden * sig * (1.0 - sig))).astype(jnp.bfloat16)
        return jnp.dot(hid_grad, w_first.T, preferred_element_type=jnp.float32)

    def block_back(grad_in):
        norm_gradient = project_all(normalized_input, grad_in)
        gain_partial = jnp.sum(norm_gradient * standardized_input, 0)
        gain_scaled = norm_gradient * gain_vector
        backward_result = inverse_deviation * (
            gain_scaled
            - jnp.mean(gain_scaled, -1, keepdims=True)
            - standardized_input * jnp.mean(gain_scaled * standardized_input, -1, keepdims=True)
        )
        return (
            (grad_in.astype(jnp.float32) + backward_result).astype(jnp.bfloat16),
            gain_partial,
        )

    def pass_through(grad_in):
        return (grad_in, jnp.zeros((width,), jnp.float32))

    segments = lax.axis_size("segment")
    my_segment = lax.axis_index("segment")
    gain_local = jnp.zeros((width,), jnp.float32)
    result = current
    for level in range(segments - 1, -1, -1):
        mine = my_segment == level
        updated, gain_partial = lax.cond(mine, block_back, pass_through, current)
        result = jnp.where(mine, updated, result)
        gain_local = jnp.where(mine, gain_partial, gain_local)
        if level > 0:
            current = passed_along(updated, "segment", -1)
    gain_total = lax.psum(gain_local, "dp")
    return (result[None], gain_total[None])


def kernel(
    segments, utts,
    x_ref, gain_ref, wst_ref, cot_ref, len_ref, out_ref, gg_ref,
    W, F, dz, xh, zb, g, gn, inv, xin, slots,
    lsem, hs, hr, os_, or_, fs, fr, ps, pr, xs, xr, ts, tr, gs, gr, rs, rr, qs, qr,
):
    D = x_ref.shape[1]
    T = x_ref.shape[0]
    depth = wst_ref.shape[2]
    FF = F.shape[1]
    blk = FF // PIECES
    R2 = 2 * T
    n_chunks = R2 // CHUNK

    s = lax.axis_index("segment")
    k = lax.axis_index("dp")
    z = k // 2
    c = k % 2
    worker = (z == 1) | (z == 2)
    helper = (z == 0) | (z == 3)
    top_seg = s == segments - 1
    zw = 1 + z // 2
    zh = 3 * (z // 2)
    zo = 3 - zw
    zoh = 3 - zh
    partner = 2 * z + (1 - c)
    sources = (zw, zh, zo, zoh)

    barrier = pltpu.get_barrier_semaphore()
    for d in range(1, 8):
        pl.semaphore_signal(
            barrier, inc=1, device_id={"dp": lax.rem(k + d, 8)}, device_id_type=MESH
        )

    @pl.when(s > 0)
    def _():
        pl.semaphore_signal(barrier, inc=1, device_id={"segment": s - 1}, device_id_type=MESH)

    @pl.when(s < segments - 1)
    def _():
        pl.semaphore_signal(barrier, inc=1, device_id={"segment": s + 1}, device_id_type=MESH)

    near = (s > 0).astype(jnp.int32) + (s < segments - 1).astype(jnp.int32)
    pl.semaphore_wait(barrier, 7 + near)

    def rows_of(zz, cc):
        return pl.ds(pl.multiple_of((2 * zz + cc) * depth, depth), depth)

    def cols_of(p):
        return pl.ds(pl.multiple_of(p * blk, blk), blk)

    def remote(src, dst, ssem, rsem, dev):
        return pltpu.make_async_remote_copy(
            src_ref=src, dst_ref=dst, send_sem=ssem, recv_sem=rsem,
            device_id=dev, device_id_type=MESH,
        )

    def own_src(p):
        return wst_ref.at[p]

    def slot(zz, cc, p):
        return W.at[p, :, rows_of(zz, cc), :]

    def to_worker(p):
        return remote(own_src(p), slot(z, c, p), hs.at[p], hr.at[p], {"dp": 2 * zw + c})

    def from_helper(p):
        return remote(slot(zh, c, p), slot(zh, c, p), hs.at[p], hr.at[p], {"dp": 2 * zh + c})

    def own_to_other(p):
        return remote(own_src(p), slot(z, c, p), os_.at[p], or_.at[p], {"dp": 2 * zo + c})

    def own_from_other(p):
        return remote(own_src(p), slot(zo, c, p), os_.at[p], or_.at[p], {"dp": 2 * zo + c})

    def fwd_to_other(p):
        return remote(slot(zh, c, p), slot(zh, c, p), fs.at[p], fr.at[p], {"dp": 2 * zo + c})

    def fwd_from_other(p):
        return remote(slot(zoh, c, p), slot(zoh, c, p), fs.at[p], fr.at[p], {"dp": 2 * zo + c})

    def to_partner(i, p):
        src = own_src(p) if i == 0 else slot(sources[i], c, p)
        return remote(src, slot(sources[i], c, p), ps.at[i, p], pr.at[i, p], {"dp": partner})

    def from_partner(i, p):
        there = slot(sources[i], 1 - c, p)
        return remote(there, there, ps.at[i, p], pr.at[i, p], {"dp": partner})

    local = pltpu.make_async_copy(wst_ref, W.at[:, :, rows_of(z, c), :], lsem)
    top_rows = g.at[pl.ds(T, T), :]
    x_send = remote(x_ref, xin.at[pl.ds(0, T), :], xs, xr, {"dp": 2 * zw + c})
    x_recv = remote(x_ref, xin.at[pl.ds(0, T), :], xs, xr, {"dp": 2 * zh + c})
    t_send = remote(top_rows, g.at[pl.ds(0, T), :], ts, tr, {"dp": 2 * zw + c})
    t_recv = remote(top_rows, g.at[pl.ds(0, T), :], ts, tr, {"dp": 2 * zh + c})
    ret_send = remote(gn.at[pl.ds(0, T), :], gn.at[pl.ds(T, T), :], rs, rr, {"dp": 2 * zh + c})
    ret_recv = remote(gn.at[pl.ds(0, T), :], gn.at[pl.ds(T, T), :], rs, rr, {"dp": 2 * zw + c})

    @pl.when(helper)
    def _():
        x_send.start()

    @pl.when(worker)
    def _():
        own_to_other(0).start()
        to_partner(0, 0).start()
        own_to_other(1).start()
        to_partner(0, 1).start()
        local.start()

    @pl.when(top_seg)
    def _():
        pos = k * T + lax.broadcasted_iota(jnp.int32, (T, 128), 0)
        tok = jnp.zeros((T, 128), jnp.float32)
        start = jnp.int32(0)
        for j in range(utts):
            n = len_ref[j]
            hit = (pos >= start) & (pos < start + n)
            tok = jnp.where(hit, n.astype(jnp.float32), tok)
            start = start + n
        weight = (2.0 * T / (tok + T))[:, 0:1]
        g[T:, :] = (cot_ref[...].astype(jnp.float32) * weight).astype(jnp.bfloat16)

    @pl.when(helper & top_seg)
    def _():
        t_send.start()

    @pl.when(helper)
    def _():
        @pl.loop(0, PIECES)
        def _(p):
            to_worker(p).start()

    NORM = 64

    @pl.when(worker)
    def _():
        xin[T:, :] = x_ref[...]
        x_recv.wait_recv()

        @pl.loop(0, R2 // NORM)
        def _(i):
            r = pl.ds(pl.multiple_of(i * NORM, NORM), NORM)
            xf = xin[r, :].astype(jnp.float32)
            cen = xf - jnp.mean(xf, -1, keepdims=True)
            iv = lax.rsqrt(jnp.mean(cen * cen, -1, keepdims=True) + 1e-05)
            xhat = cen * iv
            inv[r, :] = jnp.broadcast_to(iv, (NORM, 128))
            xh[r, :] = xhat
            zb[r, :] = (xhat * gain_ref[...]).astype(jnp.bfloat16)
            dz[r, :] = jnp.zeros((NORM, D), jnp.float32)

        @pl.when(top_seg)
        def _():
            t_recv.wait_recv()

        local.wait()

    def hidden(p):
        h = jnp.dot(zb[...], W[p, 0], preferred_element_type=jnp.float32)
        sig = jax.nn.sigmoid(h)
        F[:, cols_of(p)] = 0.5 * (sig + h * sig * (1.0 - sig))

    def back(p, r):
        u = jnp.dot(g[r, :], W[p, 1], preferred_element_type=jnp.float32)
        du = (u * F[r, cols_of(p)]).astype(jnp.bfloat16)
        dz[r, :] += lax.dot_general(
            du, W[p, 0], (((1,), (1,)), ((), ())),
            preferred_element_type=jnp.float32,
        )

    def piece(p):
        for i in range(4):
            from_partner(i, p).wait_recv()
        hidden(p)

        @pl.when(top_seg)
        def _():
            back(p, pl.ds(0, R2))

    @pl.when(worker)
    def _():
        @pl.loop(0, PIECES)
        def _(p):
            @pl.when(p + 2 < PIECES)
            def _():
                own_to_other(p + 2).start()
                to_partner(0, p + 2).start()

            from_helper(p).wait_recv()
            fwd_to_other(p).start()
            to_partner(1, p).start()
            own_from_other(p).wait_recv()
            to_partner(2, p).start()
            fwd_from_other(p).wait_recv()
            to_partner(3, p).start()
            @pl.when(p > 0)
            def _():
                piece(p - 1)

        piece(PIECES - 1)

    def g_copy(i, to):
        r = pl.ds(pl.multiple_of(i * CHUNK, CHUNK), CHUNK)
        return remote(gn.at[r, :], g.at[r, :], gs.at[i], gr.at[i], {"segment": to})

    wi = jnp.clip((z - 1) * 2 + c, 0, 3)
    EP = 64

    @pl.when(worker)
    def _():
        slots[wi] = jnp.zeros((1, D), jnp.float32)

        @pl.loop(0, n_chunks)
        def _(i):
            r = pl.ds(pl.multiple_of(i * CHUNK, CHUNK), CHUNK)

            @pl.when(jnp.logical_not(top_seg))
            def _():
                g_copy(i, s + 1).wait_recv()

                @pl.loop(0, PIECES)
                def _(p):
                    back(p, r)

            @pl.loop(0, CHUNK // EP)
            def _(j):
                q = pl.ds(pl.multiple_of(i * CHUNK + j * EP, EP), EP)
                d = dz[q, :]
                xhat = xh[q, :]
                t = d * xhat
                slots[wi] += jnp.sum(t, 0, keepdims=True)
                gain = gain_ref[...]
                e = d * gain
                m1 = jnp.mean(e, -1, keepdims=True)
                m2 = jnp.mean(t * gain, -1, keepdims=True)
                gn[q, :] = (
                    g[q, :].astype(jnp.float32) + inv[q, 0:1] * (e - m1 - xhat * m2)
                ).astype(jnp.bfloat16)

            @pl.when(s > 0)
            def _():
                g_copy(i, s - 1).start()

            @pl.when((i + 1) * CHUNK == T)
            def _():
                ret_send.start()

    def q_copy(d):
        return remote(slots.at[wi], slots.at[wi], qs.at[d], qr.at[wi], {"dp": lax.rem(k + d, 8)})

    @pl.when(worker)
    def _():
        for d in range(1, 8):
            q_copy(d).start()
        out_ref[...] = gn[T:, :]

    @pl.when(helper)
    def _():
        ret_recv.wait_recv()
        out_ref[...] = gn[T:, :]

    for w in range(4):
        @pl.when(k != w + 2)
        def _(w=w):
            remote(
                slots.at[w], slots.at[w], qs.at[0], qr.at[w], {"dp": partner}
            ).wait_recv()

    gg_ref[...] = slots[0] + slots[1] + slots[2] + slots[3]

    @pl.when(worker)
    def _():
        for d in range(1, 8):
            q_copy(d).wait_send()
        ret_send.wait_send()

        @pl.loop(0, PIECES)
        def _(p):
            own_to_other(p).wait_send()
            fwd_to_other(p).wait_send()
            for i in range(4):
                to_partner(i, p).wait_send()

        @pl.when(s > 0)
        def _():
            @pl.loop(0, n_chunks)
            def _(i):
                g_copy(i, s - 1).wait_send()

    @pl.when(helper)
    def _():
        x_send.wait_send()

        @pl.loop(0, PIECES)
        def _(p):
            to_worker(p).wait_send()

        @pl.when(top_seg)
        def _():
            t_send.wait_send()


def in_kernel(segments, x_saved, gains, w_in, w_out, cotangent, lengths):
    T, D = cotangent.shape
    FF = w_in.shape[2]
    wst = jnp.stack(
        [
            w_in[0].reshape(-1, PIECES, FF // PIECES).transpose(1, 0, 2),
            w_out[0].reshape(PIECES, FF // PIECES, -1).transpose(0, 2, 1),
        ],
        1,
    )
    R2 = 2 * T
    DMA = pltpu.SemaphoreType.DMA
    bf, f32 = jnp.bfloat16, jnp.float32
    vmem = pl.BlockSpec(memory_space=pltpu.VMEM)
    grads, gg = pl.pallas_call(
        functools.partial(kernel, segments, lengths.shape[0]),
        out_shape=(jax.ShapeDtypeStruct((T, D), bf), jax.ShapeDtypeStruct((1, D), f32)),
        in_specs=[
            vmem, vmem, pl.BlockSpec(memory_space=pl.ANY), vmem,
            pl.BlockSpec(memory_space=pltpu.SMEM),
        ],
        out_specs=(vmem, vmem),
        scratch_shapes=[
            pltpu.VMEM((PIECES, 2, D, FF // PIECES), bf),
            pltpu.VMEM((R2, FF), f32),
            pltpu.VMEM((R2, D), f32),
            pltpu.VMEM((R2, D), f32),
            pltpu.VMEM((R2, D), bf),
            pltpu.VMEM((R2, D), bf),
            pltpu.VMEM((R2, D), bf),
            pltpu.VMEM((R2, 128), f32),
            pltpu.VMEM((R2, D), bf),
            pltpu.VMEM((4, 1, D), f32),
            DMA, DMA((PIECES,)), DMA((PIECES,)), DMA((PIECES,)), DMA((PIECES,)),
            DMA((PIECES,)), DMA((PIECES,)), DMA((4, PIECES)), DMA((4, PIECES)),
            DMA, DMA, DMA, DMA, DMA((R2 // CHUNK,)), DMA((R2 // CHUNK,)),
            DMA, DMA, DMA((8,)), DMA((4,)),
        ],
        compiler_params=pltpu.CompilerParams(
            collective_id=0, has_side_effects=True, vmem_limit_bytes=56 * 1024 * 1024
        ),
    )(x_saved[0], gains, wst, cotangent, lengths)
    return (grads[None], gg)


def solution(mesh):
    in_specs = (
        P("segment", "dp", None),
        P("segment", None),
        P("segment", "dp", None),
        P("segment", None, "dp"),
        P("dp", None),
        P(),
    )
    out_specs = (P("segment", "dp", None), P("segment", None))
    body = on_device
    if mesh.shape["dp"] == 8:
        body = functools.partial(in_kernel, mesh.shape["segment"])
    return jax.shard_map(
        body, mesh=mesh, in_specs=in_specs, out_specs=out_specs, check_vma=False
    )
```
